128 devices in a mesh: dp: 4 (over y_hi, core), fsdp: 32 (over x, z, y_lo).
Axes of the slice: x: 4, y: 4 (y_hi: 2, y_lo: 2; y = y_hi * 2 + y_lo), z: 4, core: 2. Of those that a mesh axis runs over, the one named last changes fastest.
Arguments:
- normed: bfloat16 [131072, 4096], P(('dp', 'fsdp')), may hold values from -24 to 24
- k_weight: bfloat16 [4096, 512], P('fsdp'), may hold values from -0.09375 to 0.09375
- k_gain: float32 [128], replicated, may hold values from 0.5 to 1.5
- probe_k: bfloat16 [4096, 512], P('fsdp'), may hold values from -6 to 6
- probe_v: bfloat16 [4096, 512], P('fsdp'), may hold values from -6 to 6
Outputs:
- diag_k: float32 [4096, 512], P(('dp', 'fsdp'))
- diag_v: float32 [4096, 512], P(('dp', 'fsdp'))
The draws below stay inside these ranges and needn't reach their ends.
All inputs are finite; a program needn't handle non-finite values.
Results may differ from the reference program's by a relative error of at most 0.00075.
Values may be sent and summed in bfloat16 or wider, within the bound.
A program may use at most 128 MiB of HBM per device.

```python
import jax
import jax.numpy as jnp
from jax import lax

D = 4096
HEAD = 128
KV = 512
TOKENS = 131072


def strengthened(drawn, stream_key, source, target, parts, factor):
    def block_of(position):
        return (jnp.arange(drawn.shape[position]) // (drawn.shape[position] // parts)).reshape((-1,) + (1,) * (drawn.ndim - 1 - position))

    first = jax.random.permutation(stream_key, parts)[block_of(target)]
    other_side = (block_of(target) + parts // 2) % parts
    return jnp.where((block_of(source) == first) | (block_of(source) == other_side), factor * drawn, drawn)


def level_of(own_key, shape, split, low, largest):
    factor_of, own = 1.0, jax.random.fold_in(own_key, 6)
    for axis_at, parts in split:
        heights = jnp.exp(jax.random.uniform(jax.random.fold_in(own, axis_at), (parts,), jnp.float32, low / len(split), largest / len(split)))
        factor_of = factor_of * jnp.repeat(heights, shape[axis_at] // parts).reshape([-1 if axis == axis_at else 1 for axis in range(len(shape))])
    return factor_of


def scatter_about(rng, shape, scale, most, pieces=(), dtype=jnp.bfloat16):
    drawn = scale * jax.random.normal(rng, shape, jnp.float32)
    if pieces:
        drawn = drawn * level_of(rng, shape, pieces, -0.22, 0.18)
    return jnp.clip(drawn, -most, most).astype(dtype)


def heavy_noise(rng, shape, scale, reach, split, heavy, kind=jnp.bfloat16):
    entries = scale * jax.random.normal(rng, shape, jnp.float32)
    if split:
        entries = entries * level_of(rng, shape, split, -0.22, 0.18)
    return jnp.clip(strengthened(entries, jax.random.fold_in(rng, 3), *heavy), -reach, reach).astype(kind)


def setup_inputs(seed: int = 0) -> dict:
    arg_keys = jax.random.split(jax.random.key(seed), 6)
    return {
        "normed": heavy_noise(arg_keys[0], (TOKENS, D), 1.0, 24.0, ((0, 128),), (0, 1, 128, 5.5)),
        "k_weight": scatter_about(arg_keys[1], (D, KV), D ** -0.5, 0.09375, ((0, 32),)),
        "k_gain": jnp.clip(1.0 + 0.1 * jax.random.normal(arg_keys[2], (HEAD,), jnp.float32), 0.5, 1.5),
        "probe_k": scatter_about(arg_keys[3], (D, KV), 1.0, 6.0, ((0, 32),)),
        "probe_v": scatter_about(arg_keys[4], (D, KV), 1.0, 6.0, ((0, 32),)),
    }


EPS = 1e-06

def cotangent(raw, tangent_k, tangent_v, gain):
    rows = raw.shape[0]
    heads = raw.shape[1] // HEAD
    alpha = raw.reshape(rows, heads, HEAD)
    delta = tangent_k.reshape(rows, heads, HEAD)
    scale = gain.astype(jnp.float32)
    inv = lax.rsqrt(lax.optimization_barrier(jnp.mean(alpha * alpha, axis=-1, keepdims=True)) + EPS)
    cubed = inv * inv * inv
    key_tan = scale * (delta * inv - alpha * (lax.optimization_barrier(jnp.sum(alpha * delta, axis=-1, keepdims=True)) / HEAD) * cubed)
    back = scale * key_tan * inv - alpha * (lax.optimization_barrier(jnp.sum(alpha * scale * key_tan, axis=-1, keepdims=True)) / HEAD) * cubed
    return jnp.concatenate([back.reshape(rows, heads * HEAD), tangent_v], axis=1).astype(jnp.bfloat16)

def reference(normed, k_weight, k_gain, probe_k, probe_v):
    width = k_weight.shape[1]
    raw = jnp.dot(normed, k_weight, preferred_element_type=jnp.float32)
    probes = jnp.concatenate([probe_k, probe_v], axis=1)
    tangent = jnp.dot(normed, probes, preferred_element_type=jnp.float32)
    cot = cotangent(raw, tangent[:, :width], tangent[:, width:], k_gain)
    product = lax.dot_general(normed, cot, (((0,), (0,)), ((), ())), preferred_element_type=jnp.float32)
    estimate = product * probes.astype(jnp.float32) / TOKENS
    return (estimate[:, :width], estimate[:, width:])
```

```python
import jax
import jax.numpy as jnp
from jax import lax
from jax.experimental import pallas as pl
from jax.experimental.pallas import tpu as pltpu
from jax.sharding import PartitionSpec as P

HEAD = 128
EPS = 1e-06
MESH = pl.DeviceIdType.MESH
F32 = jnp.float32
BF16 = jnp.bfloat16
TOKENS = 131072
ROWS = 1024
COLS = 3 * HEAD
NT = (((1,), (1,)), ((), ()))
N_REMOTE = 30 + 8 + 4 * (6 + 3 + 3) + 4


class Place:
    def __init__(self):
        dp, fs = lax.axis_index("dp"), lax.axis_index("fsdp")
        self.c = dp % 2
        x, z = fs // 8, (fs // 2) % 4
        self.at = {
            "a": x + self.c * (z - x),
            "b": z + self.c * (x - z),
            "y": (dp // 2) * 2 + fs % 2,
        }
        self.fs = fs
        self.y_hi = dp // 2
        self.y_lo = fs % 2

    def xz(self, a, b):
        return a + self.c * (b - a), b + self.c * (a - b)

    def device(self, axis, step):
        at = dict(self.at)
        at[axis] = (at[axis] + step) % 4
        x, z = self.xz(at["a"], at["b"])
        return ((at["y"] // 2) * 2 + self.c, x * 8 + z * 2 + at["y"] % 2)

    def sibling(self):
        return (self.y_hi * 2 + 1 - self.c, self.fs)

    def shard(self, a, b, y_lo):
        x, z = self.xz(a, b)
        return x * 8 + z * 2 + y_lo

    def block(self, a, b, y, core):
        x, z = self.xz(a, b)
        return ((y // 2) * 2 + core) * 32 + x * 8 + z * 2 + y % 2


def kernel(
    normed, kw, gain, pk, pv, out_k, out_v,
    stage, xt, wt, acc, cot, part, r1, r2, r3, probes, result, landed, gcol,
    load_sem, send_sem, recv_sem,
):
    me = Place()
    a, b, y, yl, c = me.at["a"], me.at["b"], me.at["y"], me.y_lo, me.c
    count = [0]
    started = []

    def send(src, dst, device):
        k = count[0]
        count[0] += 1
        copy = pltpu.make_async_remote_copy(
            src_ref=src, dst_ref=dst, send_sem=send_sem.at[k], recv_sem=recv_sem.at[k],
            device_id=device, device_id_type=MESH,
        )
        copy.start()
        started.append(copy)
        return copy

    def same(ref, device):
        return send(ref, ref, device)

    def load(i):
        return pltpu.make_async_copy(
            normed.at[:, pl.ds(i * 512, 512)], stage.at[i % 4], load_sem.at[i % 4]
        )

    barrier = pltpu.get_barrier_semaphore()
    greeted = [me.device(axis, d) for axis in ("a", "b", "y") for d in (1, 2, 3)]
    greeted.append(me.sibling())
    for device in greeted:
        pl.semaphore_signal(barrier, inc=1, device_id=device, device_id_type=MESH)
    loads = [load(i) for i in range(8)]
    for i in range(4):
        loads[i].start()

    for h in range(2):
        cols = pl.ds(pl.multiple_of(c * 256 + h * HEAD, HEAD), HEAD)
        for j, ref in enumerate((kw, pk, pv)):
            wt[h, a, b, yl, j * HEAD:(j + 1) * HEAD, :] = ref[:, cols].T
    gcol[...] = jnp.broadcast_to(gain[...], (HEAD, HEAD)).T
    pl.semaphore_wait(barrier, len(greeted))

    h0, h1 = pl.ds(0, COLS // 2), pl.ds(COLS // 2, COLS // 2)
    am, ap, bm, bp = (a + 3) % 4, (a + 1) % 4, (b + 3) % 4, (b + 1) % 4
    ao, bo, yo = (a + 2) % 4, (b + 2) % 4, 1 - yl
    to = {(axis, d): me.device(axis, d) for axis in ("a", "b", "y") for d in (1, 2, 3)}
    AP, AM, BP, BM, YP, YM = (to[k] for k in (("a", 1), ("a", 3), ("b", 1), ("b", 3), ("y", 1), ("y", 3)))

    c0p, c0m = same(wt.at[0, a, b, yl], AP), same(wt.at[0, a, b, yl], AM)
    d0p, d0m = same(wt.at[1, a, b, yl], BP), same(wt.at[1, a, b, yl], BM)

    sibling = me.sibling()
    pair = []

    def turn(i):
        loads[i].wait()
        for j in range(4):
            k = i * 16 + j * 4
            xt[0, k:k + 4] = stage[i % 4, :, j * HEAD:(j + 1) * HEAD].T.reshape(4, 32, ROWS)
        if i + 4 < 8:
            loads[i + 4].start()
        pair.append(send(xt.at[0, pl.ds(i * 16, 16)], xt.at[1, pl.ds(i * 16, 16)], sibling))

    for i in range(4):
        turn(i)
    c0p.wait_recv()
    f0p = same(wt.at[0, am, b, yl, h0], AP)
    c0m.wait_recv()
    f0m = same(wt.at[0, ap, b, yl, h1], AM)
    d0p.wait_recv()
    g0p = same(wt.at[1, a, bm, yl, h0], BP)
    d0m.wait_recv()
    g0m = same(wt.at[1, a, bp, yl, h1], BM)
    for i in range(4, 8):
        turn(i)

    def over_y(h, b_at):
        return (same(wt.at[h, :, b_at, yl, h0], YP), same(wt.at[h, :, b_at, yl, h1], YM))

    f0p.wait_recv()
    f0m.wait_recv()
    c1p, c1m = same(wt.at[0, :, b, yl], BP), same(wt.at[0, :, b, yl], BM)
    g0p.wait_recv()
    g0m.wait_recv()
    e0p, e0m = same(wt.at[1, a, :, yl, h0], YP), same(wt.at[1, a, :, yl, h1], YM)
    s0p, s0m = same(wt.at[1, a, :, yl], AP), same(wt.at[1, a, :, yl], AM)
    y0 = over_y(0, b)

    def piece(h, halves, shards, first=False):
        @pl.loop(0, 2 * len(halves))
        def _(n):
            half = n // 2 if len(halves) == 2 else halves[0]
            at = pl.ds(pl.multiple_of((n % 2) * 512, 512), 512)
            lhs = jnp.concatenate([wt[h, i, j, k] for i, j, k in shards], axis=1)
            rhs = jnp.concatenate(
                [xt[half, pl.ds(4 * me.shard(i, j, k), 4), :, at].reshape(HEAD, 512) for i, j, k in shards], axis=0
            )
            new = jnp.dot(lhs, rhs, preferred_element_type=F32)
            if first:
                acc[h, half, :, at] = new
            else:
                acc[h, half, :, at] += new

    every = range(4)
    piece(0, (0,), [(i, b, yl) for i in every], first=True)
    piece(1, (0,), [(a, j, yl) for j in every], first=True)
    e0p.wait_recv()
    e0m.wait_recv()
    s1p, s1m = same(wt.at[1, a, :, yo], AP), same(wt.at[1, a, :, yo], AM)
    piece(1, (0,), [(a, j, yo) for j in every])
    c1p.wait_recv()
    f1p = same(wt.at[0, :, bm, yl, h0], BP)
    y1 = over_y(0, bm)
    c1m.wait_recv()
    f1m = same(wt.at[0, :, bp, yl, h1], BM)
    y2 = over_y(0, bp)
    for copy in y0:
        copy.wait_recv()
    piece(0, (0,), [(i, b, yo) for i in every])
    s0p.wait_recv()
    t0p = same(wt.at[1, am, :, yl, h0], AP)
    s0m.wait_recv()
    t0m = same(wt.at[1, ap, :, yl, h1], AM)
    piece(1, (0,), [(i, j, yl) for i in (am, ap) for j in every])
    f1p.wait_recv()
    f1m.wait_recv()
    y3 = over_y(0, bo)
    piece(0, (0,), [(i, j, yl) for i in every for j in (bm, bp)])
    s1p.wait_recv()
    t1p = same(wt.at[1, am, :, yo, h0], AP)
    s1m.wait_recv()
    t1m = same(wt.at[1, ap, :, yo, h1], AM)
    for copy in pair:
        copy.wait_recv()
    piece(1, (1,), [(a, j, k) for j in every for k in (yl, yo)]
          + [(i, j, yl) for i in (am, ap) for j in every], first=True)
    piece(0, (1,), [(i, b, k) for i in every for k in (yl, yo)]
          + [(i, j, yl) for i in every for j in (bm, bp)], first=True)
    piece(1, (0, 1), [(i, j, yo) for i in (am, ap) for j in every])
    for copy in y1 + y2:
        copy.wait_recv()
    piece(0, (0, 1), [(i, j, yo) for i in every for j in (bm, bp)])
    for copy in (t0p, t0m, t1p, t1m):
        copy.wait_recv()
    piece(1, (0, 1), [(ao, j, k) for j in every for k in (yl, yo)])
    for copy in y3:
        copy.wait_recv()
    piece(0, (0, 1), [(i, bo, k) for i in every for k in (yl, yo)])

    for h in range(2):
        for half in range(2):
            cot[h * HEAD:(h + 1) * HEAD, half * ROWS:(half + 1) * ROWS] = (
                acc[h, half, 2 * HEAD:3 * HEAD, :].astype(BF16)
            )

    def cot_k(h):
        @pl.loop(0, 16)
        def _(n):
            half = n // 8
            at = pl.ds(pl.multiple_of((n % 8) * HEAD, HEAD), HEAD)
            alpha = acc[h, half, 0:HEAD, at]
            delta = acc[h, half, HEAD:2 * HEAD, at]
            g = gcol[...]
            inv = lax.rsqrt(jnp.mean(alpha * alpha, axis=0, keepdims=True) + EPS)
            cubed = inv * inv * inv
            along = jnp.sum(alpha * delta, axis=0, keepdims=True) / HEAD
            gt = g * (g * (delta * inv - alpha * (along * cubed)))
            back = gt * inv - alpha * ((jnp.sum(alpha * gt, axis=0, keepdims=True) / HEAD) * cubed)
            cot[(2 + h) * HEAD:(3 + h) * HEAD, pl.ds(pl.multiple_of(n * HEAD, HEAD), HEAD)] = back.astype(BF16)

    axes = (("a", "y", "b"), ("y", "a", "b"), ("b", "y", "a"), ("a", "y", "b"))
    first = [{} for _ in axes]

    def spot(q, at):
        i, j, k = (at[axis] for axis in axes[q])
        return i * 16 + j * 4 + k

    def tile(pair_at, at1, at2, i1, i2):
        third = next(axis for axis in ("a", "b", "y") if axis not in (at1, at2))
        spots = [{at1: i1, at2: i2, third: k} for k in every]
        blocks = [me.block(s["a"], s["b"], s["y"], core) for s in spots for core in range(2)]
        lhs = jnp.concatenate(
            [jnp.concatenate([xt[half, k] for k in blocks], axis=0) for half in range(2)], axis=1
        )
        new = lax.dot_general(
            lhs, cot[pl.ds(pair_at * 2 * HEAD, 2 * HEAD), :], NT, preferred_element_type=F32
        )
        for n, s in enumerate(spots):
            for q in range(2):
                part[2 * pair_at + q, spot(2 * pair_at + q, s)] = (
                    new[n * 64:(n + 1) * 64, q * HEAD:(q + 1) * HEAD]
                )

    def half_of(q, step, half):
        return part.at[q, pl.ds(((me.at[axes[q][0]] + step) % 4) * 16 + half * 8, 8)]

    def far(q):
        axis = axes[q][0]
        first[q][0] = send(half_of(q, 2, 0), r1.at[q, 0], to[axis, 1])
        first[q][1] = send(half_of(q, 2, 1), r1.at[q, 1], to[axis, 3])

    def near_plus(q):
        first[q][2] = send(half_of(q, 1, 1), r1.at[q, 2], to[axes[q][0], 1])

    def near_minus(q):
        first[q][3] = send(half_of(q, 3, 0), r1.at[q, 3], to[axes[q][0], 3])

    def add(q, step, half, slots):
        base = ((me.at[axes[q][0]] + step) % 4) * 16 + half * 8
        for slot in slots:
            first[q][slot].wait_recv()

        @pl.loop(0, 8)
        def _(n):
            total = part[q, base + n]
            for slot in slots:
                total = total + r1[q, slot, n]
            part[q, base + n] = total

    def relay(q):
        axis = axes[q][0]
        add(q, 1, 0, (0,))
        first[q][4] = send(half_of(q, 1, 0), r1.at[q, 4], to[axis, 1])
        add(q, 3, 1, (1,))
        first[q][5] = send(half_of(q, 3, 1), r1.at[q, 5], to[axis, 3])

    def product(pair_at, q1, q2):
        at1, at2 = axes[q1][0], axes[q2][0]
        m1, m2 = me.at[at1], me.at[at2]

        @pl.loop(0, 4)
        def _(n):
            tile(pair_at, at1, at2, (m1 + 2) % 4, (m2 + 2 + n) % 4)

        far(q1)

        @pl.loop(0, 3)
        def _(n):
            tile(pair_at, at1, at2, (m1 + 3 + n) % 4, (m2 + 2) % 4)

        far(q2)

        @pl.loop(0, 3)
        def _(n):
            tile(pair_at, at1, at2, (m1 + 1) % 4, (m2 + 3 + n) % 4)

        near_plus(q1)

        @pl.loop(0, 3)
        def _(n):
            tile(pair_at, at1, at2, (m1 + 3) % 4, (m2 + 3 + n) % 4)

        near_minus(q1)

        @pl.loop(0, 3)
        def _(n):
            tile(pair_at, at1, at2, m1, (m2 + 3 + n) % 4)

        near_plus(q2)
        near_minus(q2)

    def second(q):
        add(q, 0, 0, (3, 4))
        add(q, 0, 1, (2, 5))
        i, j = me.at[axes[q][0]], me.at[axes[q][1]]
        return [
            send(part.at[q, pl.ds(i * 16 + ((j + d) % 4) * 4, 4)], r2.at[q, d - 1], to[axes[q][1], d])
            for d in (2, 1, 3)
        ]

    def third(q, copies):
        i, j, k = (me.at[axis] for axis in axes[q])
        for copy in copies:
            copy.wait_recv()
        base = i * 16 + j * 4

        @pl.loop(0, 4)
        def _(n):
            part[q, base + n] = part[q, base + n] + r2[q, 0, n] + r2[q, 1, n] + r2[q, 2, n]

        return [
            send(part.at[q, base + (k + d) % 4], r3.at[q, d - 1], to[axes[q][2], d]) for d in (2, 1, 3)
        ]

    def last(q, copies):
        for copy in copies:
            copy.wait_recv()
        total = part[q, spot(q, me.at)] + r3[q, 0] + r3[q, 1] + r3[q, 2]
        result[q] = (total * probes[q]) * (1.0 / TOKENS)
        return send(result.at[q, pl.ds(pl.multiple_of((1 - c) * 32, 32), 32)], landed.at[q], sibling)

    product(0, 0, 1)
    cot_k(0)
    cot_k(1)
    relay(0)
    relay(1)
    product(1, 3, 2)
    relay(3)
    relay(2)

    for core in range(2):
        s = (me.y_hi * 2 + core) * 8 + me.fs // 4
        i, j = me.xz(s // 8, (s // 2) % 4)
        for q in range(4):
            h, row = q % 2, (2 * HEAD if q < 2 else HEAD)
            gcol[...] = wt[h, i, j, s % 2, row:row + HEAD, :].T.astype(F32)
            probes[q, core * 32:(core + 1) * 32] = gcol[pl.ds(pl.multiple_of((me.fs % 4) * 32, 32), 32), :]

    s = [None] * 4
    t = [None] * 4
    for q in (0, 1, 3, 2):
        s[q] = second(q)
    for q in (0, 1, 3, 2):
        t[q] = third(q, s[q])
    final = [None] * 4
    for q in (0, 1, 3, 2):
        final[q] = last(q, t[q])
    for q in range(4):
        out = out_v if q < 2 else out_k
        mine = pl.ds(pl.multiple_of(c * 256 + (q % 2) * HEAD, HEAD), HEAD)
        theirs = pl.ds(pl.multiple_of((1 - c) * 256 + (q % 2) * HEAD, HEAD), HEAD)
        out[:, mine] = result[q, pl.ds(pl.multiple_of(c * 32, 32), 32), :]
        final[q].wait_recv()
        out[:, theirs] = landed[q]
    for copy in started:
        copy.wait_send()
    assert count[0] == N_REMOTE


def shards(normed, k_weight, k_gain, probe_k, probe_v):
    vmem = pl.BlockSpec(memory_space=pltpu.VMEM)
    out = jax.ShapeDtypeStruct((32, 512), F32)
    return pl.pallas_call(
        kernel,
        name="curvature",
        out_shape=(out, out),
        in_specs=[pl.BlockSpec(memory_space=pl.ANY)] + [vmem] * 4,
        out_specs=(vmem, vmem),
        scratch_shapes=[
            pltpu.VMEM((4, ROWS, 512), BF16),
            pltpu.VMEM((2, 128, 32, ROWS), BF16),
            pltpu.VMEM((2, 4, 4, 2, COLS, HEAD), BF16),
            pltpu.VMEM((2, 2, COLS, ROWS), F32),
            pltpu.VMEM((4 * HEAD, 2 * ROWS), BF16),
            pltpu.VMEM((4, 64, 64, HEAD), F32),
            pltpu.VMEM((4, 6, 8, 64, HEAD), F32),
            pltpu.VMEM((4, 3, 4, 64, HEAD), F32),
            pltpu.VMEM((4, 3, 64, HEAD), F32),
            pltpu.VMEM((4, 64, HEAD), F32),
            pltpu.VMEM((4, 64, HEAD), F32),
            pltpu.VMEM((4, 32, HEAD), F32),
            pltpu.VMEM((HEAD, HEAD), F32),
            pltpu.SemaphoreType.DMA((4,)),
            pltpu.SemaphoreType.DMA((N_REMOTE,)),
            pltpu.SemaphoreType.DMA((N_REMOTE,)),
        ],
        compiler_params=pltpu.CompilerParams(
            collective_id=0, has_side_effects=True, vmem_limit_bytes=58 * 2**20
        ),
        cost_estimate=pl.CostEstimate(flops=21 * 10**9, bytes_accessed=10**7, transcendentals=0),
    )(normed, k_weight, k_gain.reshape(1, HEAD), probe_k, probe_v)


def solution(mesh):
    return jax.shard_map(
        shards,
        mesh=mesh,
        in_specs=(P(("dp", "fsdp"), None), P("fsdp", None), P(), P("fsdp", None), P("fsdp", None)),
        out_specs=(P(("dp", "fsdp"), None), P(("dp", "fsdp"), None)),
        check_vma=False,
    )
```

```python
import jax
import jax.numpy as jnp
from jax import lax
from jax.experimental import pallas as pl
from jax.experimental.pallas import tpu as pltpu
from jax.sharding import PartitionSpec as P

HEAD = 128
EPS = 1e-06
MESH = pl.DeviceIdType.MESH
F32 = jnp.float32
BF16 = jnp.bfloat16
TOKENS = 131072
ROWS = 1024
NT = (((1,), (1,)), ((), ()))
N_REMOTE = 56 + 8 + 4 * (6 + 3 + 3) + 4


class Place:
    def __init__(self):
        dp, fs = lax.axis_index("dp"), lax.axis_index("fsdp")
        self.c = dp % 2
        x, z = fs // 8, (fs // 2) % 4
        self.at = {
            "a": x + self.c * (z - x),
            "b": z + self.c * (x - z),
            "y": (dp // 2) * 2 + fs % 2,
        }
        self.fs = fs
        self.y_hi = dp // 2
        self.y_lo = fs % 2

        self.sa, self.sb = 8 - 6 * self.c, 2 + 6 * self.c

    def xz(self, a, b):
        return a + self.c * (b - a), b + self.c * (a - b)

    def device(self, axis, step):
        at = dict(self.at)
        at[axis] = (at[axis] + step) % 4
        x, z = self.xz(at["a"], at["b"])
        return ((at["y"] // 2) * 2 + self.c, x * 8 + z * 2 + at["y"] % 2)

    def sibling(self):
        return (self.y_hi * 2 + 1 - self.c, self.fs)

    def shard(self, a, b, y_lo):
        return a * self.sa + b * self.sb + y_lo

    def block(self, a, b, y, core):
        return a * self.sa + b * self.sb + ((y // 2) * 64 + y % 2) + core * 32


GROUP = 32
MIDDLE = 15500 / 128
SHIFT = 121.0


def encode(x, ref):
    groups = x.shape[0] // GROUP
    x = x.reshape(groups, GROUP, HEAD)
    top = jnp.maximum(jnp.max(jnp.abs(x), axis=1) * 1.01, 1e-30).astype(BF16)
    steps = MIDDLE / top.astype(F32)
    u = x * steps[:, None, :] + MIDDLE
    k = jnp.floor(u)
    code = (jnp.exp2(k - SHIFT) * (1.0 + (u - k))).astype(BF16)
    ref[0:groups * GROUP, :] = code.reshape(groups * GROUP, HEAD)
    if groups < 16:
        top = jnp.concatenate([top.astype(F32), jnp.zeros((16 - groups, HEAD), F32)], axis=0).astype(BF16)
    ref[groups * GROUP:groups * GROUP + 16, :] = top


def decode(ref, rows):
    groups = rows // GROUP
    y = ref[0:rows, :].astype(F32).reshape(groups, GROUP, HEAD)
    top = ref[rows:rows + 16, :].astype(F32)[0:groups] * (1.0 / MIDDLE)
    k = jnp.floor(jnp.log2(y * (1.0 + 1.0 / 512.0)))
    u = (k + (SHIFT - 1.0 - MIDDLE)) + y * jnp.exp2(-k)
    return (u * top[:, None, :]).reshape(rows, HEAD)


def kernel(
    normed, kw, gain, pk, pv, out_k, out_v,
    stage, xt, wk, wv, acc, cot, part, o1, r1, o2, r2, r3, probes, result, landed, gcol,
    load_sem, send_sem, recv_sem,
):
    me = Place()
    a, b, yl, c = me.at["a"], me.at["b"], me.y_lo, me.c
    every = range(4)
    count = [0]
    started = []

    def send(src, dst, device, now=True):
        k = count[0]
        count[0] += 1
        copy = pltpu.make_async_remote_copy(
            src_ref=src, dst_ref=dst, send_sem=send_sem.at[k], recv_sem=recv_sem.at[k],
            device_id=device, device_id_type=MESH,
        )
        started.append(copy)
        if now:
            copy.start()
        return copy

    def same(ref, device):
        return send(ref, ref, device)

    def arrive(*copies):
        for copy in copies:
            copy.wait_recv()

    def load(i):
        return pltpu.make_async_copy(
            normed.at[:, pl.ds(i * 512, 512)], stage.at[i % 4], load_sem.at[i % 4]
        )

    barrier = pltpu.get_barrier_semaphore()
    greeted = [me.device(axis, d) for axis in ("a", "b", "y") for d in (1, 2, 3)]
    greeted.append(me.sibling())
    for device in greeted:
        pl.semaphore_signal(barrier, inc=1, device_id=device, device_id_type=MESH)
    loads = [load(i) for i in range(8)]
    for i in range(4):
        loads[i].start()

    to = {(axis, d): me.device(axis, d) for axis in ("a", "b", "y") for d in (1, 2, 3)}
    AP, AM, BP, BM, YP, YM = (to[k] for k in (("a", 1), ("a", 3), ("b", 1), ("b", 3), ("y", 1), ("y", 3)))
    am, ap, bm, bp = (a + 3) % 4, (a + 1) % 4, (b + 3) % 4, (b + 1) % 4
    ao, bo, yo = (a + 2) % 4, (b + 2) % 4, 1 - yl
    sibling = me.sibling()

    class Gather:
        def __init__(self, w, rows):
            self.w = w
            self.h0, self.h1 = pl.ds(0, rows // 2), pl.ds(rows // 2, rows // 2)

        def over_y(self, at):
            w = self.w
            return same(w.at[0, :, at, yl, self.h0], YP), same(w.at[0, :, at, yl, self.h1], YM)

        def start(self):
            w = self.w
            self.c0 = [same(w.at[0, a, b, yl], to["a", d]) for d in (2, 1, 3)]
            self.d0 = [same(w.at[1, a, b, yl], to["b", d]) for d in (2, 1, 3)]

        def second(self):
            w = self.w
            arrive(*self.c0)
            self.c1 = same(w.at[0, :, b, yl], BP), same(w.at[0, :, b, yl], BM)
            arrive(*self.d0)
            self.e0 = same(w.at[1, a, :, yl, self.h0], YP), same(w.at[1, a, :, yl, self.h1], YM)
            self.y0 = self.over_y(b)
            self.s0 = same(w.at[1, a, :, yl], AP), same(w.at[1, a, :, yl], AM)

        def after_e0(self):
            w = self.w
            arrive(*self.e0)
            self.s1 = same(w.at[1, a, :, yo], AP), same(w.at[1, a, :, yo], AM)

        def after_c1(self):
            w = self.w
            arrive(self.c1[0])
            f0 = same(w.at[0, :, bm, yl, self.h0], BP)
            arrive(self.c1[1])
            f1 = same(w.at[0, :, bp, yl, self.h1], BM)
            self.f1 = f0, f1
            self.y1 = self.over_y(bm) + self.over_y(bp)

        def after_s(self, k):
            w = self.w
            copies, at = (self.s0, yl) if k == 0 else (self.s1, yo)
            arrive(copies[0])
            t0 = same(w.at[1, am, :, at, self.h0], AP)
            arrive(copies[1])
            t1 = same(w.at[1, ap, :, at, self.h1], AM)
            if k == 0:
                self.t0 = t0, t1
            else:
                self.t1 = t0, t1

        def after_f1(self):
            arrive(*self.f1)
            self.y2 = self.over_y(bo)

    keys, values = Gather(wk, 2 * HEAD), Gather(wv, HEAD)

    for h in range(2):
        cols = pl.ds(pl.multiple_of(c * 256 + h * HEAD, HEAD), HEAD)
        wk[h, a, b, yl, 0:HEAD, :] = kw[:, cols].T
        wk[h, a, b, yl, HEAD:2 * HEAD, :] = pk[:, cols].T
    pl.semaphore_wait(barrier, len(greeted))
    keys.start()

    pair = []

    def turn(i):
        loads[i].wait()
        for j in range(4):
            k = i * 16 + j * 4
            xt[0, k:k + 4] = stage[i % 4, :, j * HEAD:(j + 1) * HEAD].T.reshape(4, 32, ROWS)
        if i + 4 < 8:
            loads[i + 4].start()
        pair.append(send(xt.at[0, pl.ds(i * 16, 16)], xt.at[1, pl.ds(i * 16, 16)], sibling))

    for h in range(2):
        cols = pl.ds(pl.multiple_of(c * 256 + h * HEAD, HEAD), HEAD)
        wv[h, a, b, yl] = pv[:, cols].T
    gcol[...] = jnp.broadcast_to(gain[...], (HEAD, HEAD)).T
    for i in range(4):
        turn(i)
    keys.second()
    values.start()
    for i in range(4, 8):
        turn(i)

    def piece(h, halves, shards, first=False):
        @pl.loop(0, 2 * len(halves))
        def _(n):
            half = n // 2 if len(halves) == 2 else halves[0]
            at = pl.ds(pl.multiple_of((n % 2) * 512, 512), 512)
            lhs = jnp.concatenate([wk[h, i, j, k] for i, j, k in shards], axis=1)
            rhs = jnp.concatenate(
                [xt[half, pl.ds(4 * me.shard(i, j, k), 4), :, at].reshape(HEAD, 512) for i, j, k in shards], axis=0
            )
            new = jnp.dot(lhs, rhs, preferred_element_type=F32)
            if first:
                acc[h, half, :, at] = new
            else:
                acc[h, half, :, at] += new

    piece(0, (0,), [(i, b, yl) for i in every], first=True)
    piece(1, (0,), [(a, j, yl) for j in every], first=True)
    keys.after_e0()
    keys.after_c1()
    values.second()
    keys.after_s(0)
    piece(1, (0,), [(a, j, yo) for j in every])
    arrive(*keys.y0)
    piece(0, (0,), [(i, b, yo) for i in every])
    keys.after_f1()
    keys.after_s(1)
    values.after_e0()
    values.after_c1()
    piece(1, (0,), [(i, j, yl) for i in (am, ap) for j in every])
    piece(0, (0,), [(i, j, yl) for i in every for j in (bm, bp)])
    arrive(*pair)
    piece(1, (1,), [(a, j, k) for j in every for k in (yl, yo)]
          + [(i, j, yl) for i in (am, ap) for j in every], first=True)
    values.after_s(0)
    values.after_f1()
    values.after_s(1)
    piece(0, (1,), [(i, b, k) for i in every for k in (yl, yo)]
          + [(i, j, yl) for i in every for j in (bm, bp)], first=True)
    piece(1, (0, 1), [(i, j, yo) for i in (am, ap) for j in every])
    arrive(*keys.y1)
    piece(0, (0, 1), [(i, j, yo) for i in every for j in (bm, bp)])
    arrive(*keys.t0, *keys.t1)
    piece(1, (0, 1), [(ao, j, k) for j in every for k in (yl, yo)])
    arrive(*keys.y2)
    piece(0, (0, 1), [(i, bo, k) for i in every for k in (yl, yo)])

    def cot_k():
        @pl.loop(0, 8)
        def _(n):
            at = pl.ds(pl.multiple_of((n % 4) * 256, 256), 256)
            for h in range(2):
                alpha = acc[h, n // 4, 0:HEAD, at]
                delta = acc[h, n // 4, HEAD:2 * HEAD, at]
                g = jnp.concatenate([gcol[...]] * 2, axis=1)
                inv = lax.rsqrt(jnp.mean(alpha * alpha, axis=0, keepdims=True) + EPS)
                cubed = inv * inv * inv
                along = jnp.sum(alpha * delta, axis=0, keepdims=True) / HEAD
                gt = g * (g * (delta * inv - alpha * (along * cubed)))
                back = gt * inv - alpha * ((jnp.sum(alpha * gt, axis=0, keepdims=True) / HEAD) * cubed)
                cot[(2 + h) * HEAD:(3 + h) * HEAD, pl.ds(pl.multiple_of(n * 256, 256), 256)] = back.astype(BF16)

    def cot_v():
        @pl.loop(0, 4)
        def _(n):
            lhs = jnp.concatenate(
                [
                    jnp.concatenate([wv[h, i, j, k] for s in range(16) for i, j in (me.xz(s // 4, s % 4),) for k in range(2)], axis=1)
                    for h in range(2)
                ],
                axis=0,
            )
            rhs = xt[n // 2, :, :, pl.ds(pl.multiple_of((n % 2) * 512, 512), 512)].reshape(32 * HEAD, 512)
            new = jnp.dot(lhs, rhs, preferred_element_type=F32)
            cot[0:2 * HEAD, pl.ds(pl.multiple_of(n * 512, 512), 512)] = new.astype(BF16)

    axes = (("a", "y", "b"), ("a", "b", "y"), ("a", "y", "b"), ("y", "a", "b"))
    first = [{} for _ in axes]

    def spot(q, at):
        i, j, k = (at[axis] for axis in axes[q])
        return i * 16 + j * 4 + k

    def tile(q1, q2, i1):
        spots = [dict(zip(axes[q1], (i1, j, k))) for j in every for k in every]
        blocks = [me.block(s["a"], s["b"], s["y"], core) for s in spots for core in range(2)]
        lhs = jnp.concatenate(
            [jnp.concatenate([xt[half, k] for k in blocks], axis=0) for half in range(2)], axis=1
        )
        low = min(q1, q2)
        new = lax.dot_general(lhs, cot[low * HEAD:(low + 2) * HEAD, :], NT, preferred_element_type=F32)
        for n, s in enumerate(spots):
            for q in (low, low + 1):
                part[q, spot(q, s)] = new[n * 64:(n + 1) * 64, (q - low) * HEAD:(q - low + 1) * HEAD]

    def base(q, step, half):
        return ((me.at[axes[q][0]] + step) % 4) * 16 + half * 8

    plan = ((2, 0, 1), (2, 1, 3), (1, 1, 1), (3, 0, 3), (1, 0, 1), (3, 1, 3))

    def ready(q):
        for slot, (step, half, way) in enumerate(plan):
            first[q][slot] = send(o1.at[q, slot], r1.at[q, slot], to[axes[q][0], way], now=False)

    def ship(q, slot, incoming=None):
        step, half, way = plan[slot]
        x = part[q, pl.ds(base(q, step, half), 8)].reshape(512, HEAD)
        if incoming is not None:
            x = x + decode(r1.at[q, incoming], 512)
        encode(x, o1.at[q, slot])
        first[q][slot].start()

    def product(q1, q2):
        ready(q1)
        ready(q2)
        mine = me.at[axes[q1][0]]
        along = (q1, q2) if axes[q1][0] == axes[q2][0] else (q1,)

        @pl.loop(0, 4)
        def _(n):
            tile(q1, q2, (mine + 2 + 3 * n + (n // 2) * (3 + 2 * (n % 2))) % 4)

            @pl.when(n == 0)
            def _():
                for q in along:
                    ship(q, 0)
                    ship(q, 1)

            @pl.when(n == 1)
            def _():
                for q in along:
                    ship(q, 2)

            @pl.when(n == 2)
            def _():
                for q in along:
                    ship(q, 3)

        if len(along) == 1:
            for slot in range(4):
                ship(q2, slot)

    def relay(q):
        first[q][0].wait_recv()
        ship(q, 4, 0)
        first[q][1].wait_recv()
        ship(q, 5, 1)

    s = [None] * 4
    t = [None] * 4
    final = [None] * 4

    def second(q):
        for half, slots in ((0, (3, 4)), (1, (2, 5))):
            at = pl.ds(base(q, 0, half), 8)
            total = part[q, at].reshape(512, HEAD)
            for slot in slots:
                first[q][slot].wait_recv()
                total = total + decode(r1.at[q, slot], 512)
            part[q, at] = total.reshape(8, 64, HEAD)
        i, j = me.at[axes[q][0]], me.at[axes[q][1]]
        s[q] = []
        for d in (2, 1, 3):
            encode(part[q, pl.ds(i * 16 + ((j + d) % 4) * 4, 4)].reshape(256, HEAD), o2.at[q, d - 1])
            s[q].append(send(o2.at[q, d - 1], r2.at[q, d - 1], to[axes[q][1], d]))

    def third(q):
        i, j, k = (me.at[axis] for axis in axes[q])
        at = pl.ds(i * 16 + j * 4, 4)
        total = part[q, at].reshape(256, HEAD)
        for n, d in enumerate((2, 1, 3)):
            s[q][n].wait_recv()
            total = total + decode(r2.at[q, d - 1], 256)
        part[q, at] = total.reshape(4, 64, HEAD)
        t[q] = [
            send(part.at[q, i * 16 + j * 4 + (k + d) % 4], r3.at[q, d - 1], to[axes[q][2], d]) for d in (2, 1, 3)
        ]

    def last(q):
        arrive(*t[q])
        total = part[q, spot(q, me.at)] + r3[q, 0] + r3[q, 1] + r3[q, 2]
        result[q] = (total * probes[q]) * (1.0 / TOKENS)
        final[q] = send(result.at[q, pl.ds(pl.multiple_of((1 - c) * 32, 32), 32)], landed.at[q], sibling)

    cot_k()
    product(2, 3)
    arrive(*values.y0, *values.y1, *values.y2, *values.t0, *values.t1)
    cot_v()
    relay(2)
    product(1, 0)
    relay(3)
    second(2)
    relay(1)
    relay(0)

    for core in range(2):
        n = (me.y_hi * 2 + core) * 8 + me.fs // 4
        i, j = me.xz(n // 8, (n // 2) % 4)
        for q in range(4):
            turned = wv[q, i, j, n % 2] if q < 2 else wk[q - 2, i, j, n % 2, HEAD:2 * HEAD, :]
            gcol[...] = turned.T.astype(F32)
            probes[q, core * 32:(core + 1) * 32] = gcol[pl.ds(pl.multiple_of((me.fs % 4) * 32, 32), 32), :]

    second(3)
    third(2)
    second(1)
    second(0)
    third(3)
    last(2)
    third(1)
    third(0)
    last(3)
    last(1)
    last(0)
    for q in range(4):
        out = out_v if q < 2 else out_k
        mine = pl.ds(pl.multiple_of(c * 256 + (q % 2) * HEAD, HEAD), HEAD)
        theirs = pl.ds(pl.multiple_of((1 - c) * 256 + (q % 2) * HEAD, HEAD), HEAD)
        out[:, mine] = result[q, pl.ds(pl.multiple_of(c * 32, 32), 32), :]
        final[q].wait_recv()
        out[:, theirs] = landed[q]
    for copy in started:
        copy.wait_send()
    assert count[0] == N_REMOTE


def shards(normed, k_weight, k_gain, probe_k, probe_v):
    vmem = pl.BlockSpec(memory_space=pltpu.VMEM)
    out = jax.ShapeDtypeStruct((32, 512), F32)
    return pl.pallas_call(
        kernel,
        name="curvature",
        out_shape=(out, out),
        in_specs=[pl.BlockSpec(memory_space=pl.ANY)] + [vmem] * 4,
        out_specs=(vmem, vmem),
        scratch_shapes=[
            pltpu.VMEM((4, ROWS, 512), BF16),
            pltpu.VMEM((2, 128, 32, ROWS), BF16),
            pltpu.VMEM((2, 4, 4, 2, 2 * HEAD, HEAD), BF16),
            pltpu.VMEM((2, 4, 4, 2, HEAD, HEAD), BF16),
            pltpu.VMEM((2, 2, 2 * HEAD, ROWS), F32),
            pltpu.VMEM((4 * HEAD, 2 * ROWS), BF16),
            pltpu.VMEM((4, 64, 64, HEAD), F32),
            pltpu.VMEM((4, 6, 528, HEAD), BF16),
            pltpu.VMEM((4, 6, 528, HEAD), BF16),
            pltpu.VMEM((4, 3, 272, HEAD), BF16),
            pltpu.VMEM((4, 3, 272, HEAD), BF16),
            pltpu.VMEM((4, 3, 64, HEAD), F32),
            pltpu.VMEM((4, 64, HEAD), F32),
            pltpu.VMEM((4, 64, HEAD), F32),
            pltpu.VMEM((4, 32, HEAD), F32),
            pltpu.VMEM((HEAD, HEAD), F32),
            pltpu.SemaphoreType.DMA((4,)),
            pltpu.SemaphoreType.DMA((N_REMOTE,)),
            pltpu.SemaphoreType.DMA((N_REMOTE,)),
        ],
        compiler_params=pltpu.CompilerParams(
            collective_id=0, has_side_effects=True, vmem_limit_bytes=58 * 2**20
        ),
        cost_estimate=pl.CostEstimate(flops=21 * 10**9, bytes_accessed=10**7, transcendentals=0),
    )(normed, k_weight, k_gain.reshape(1, HEAD), probe_k, probe_v)


def solution(mesh):
    return jax.shard_map(
        shards,
        mesh=mesh,
        in_specs=(P(("dp", "fsdp"), None), P("fsdp", None), P(), P("fsdp", None), P("fsdp", None)),
        out_specs=(P(("dp", "fsdp"), None), P(("dp", "fsdp"), None)),
        check_vma=False,
    )
```

```python
import jax
import jax.numpy as jnp
from jax import lax
from jax.experimental import pallas as pl
from jax.experimental.pallas import tpu as pltpu
from jax.sharding import PartitionSpec as P

HEAD = 128
EPS = 1e-06
MESH = pl.DeviceIdType.MESH
F32 = jnp.float32
BF16 = jnp.bfloat16
TOKENS = 131072
ROWS = 1024
N_REMOTE = 56 + 4 + 4 * (6 + 3 + 3 + 4) + 1


class Place:
    def __init__(self):
        dp, fs = lax.axis_index("dp"), lax.axis_index("fsdp")
        self.c = dp % 2
        x, z = fs // 8, (fs // 2) % 4
        self.at = {
            "a": x + self.c * (z - x),
            "b": z + self.c * (x - z),
            "y": (dp // 2) * 2 + fs % 2,
        }
        self.fs = fs
        self.y_hi = dp // 2
        self.y_lo = fs % 2

        self.sa, self.sb = 8 - 6 * self.c, 2 + 6 * self.c

    def xz(self, a, b):
        return a + self.c * (b - a), b + self.c * (a - b)

    def device(self, axis, step, other=False):
        at = dict(self.at)
        at[axis] = (at[axis] + step) % 4
        x, z = self.xz(at["a"], at["b"])
        core = 1 - self.c if other else self.c
        return ((at["y"] // 2) * 2 + core, x * 8 + z * 2 + at["y"] % 2)

    def sibling(self):
        return (self.y_hi * 2 + 1 - self.c, self.fs)

    def shard(self, a, b, y_lo):
        return a * self.sa + b * self.sb + y_lo

    def block(self, a, b, y, core):
        return a * self.sa + b * self.sb + ((y // 2) * 64 + y % 2) + core * 32


GROUP = 32
MIDDLE = 15500 / 128
SHIFT = 121.0


def encode(x, ref):
    groups = x.shape[0] // GROUP
    x = x.reshape(groups, GROUP, HEAD)
    top = jnp.maximum(jnp.max(jnp.abs(x), axis=1) * 1.01, 1e-30).astype(BF16)
    steps = MIDDLE / top.astype(F32)
    u = x * steps[:, None, :] + MIDDLE
    k = jnp.floor(u)
    code = (jnp.exp2(k - SHIFT) * (1.0 + (u - k))).astype(BF16)
    ref[0:groups * GROUP, :] = code.reshape(groups * GROUP, HEAD)
    if groups < 16:
        top = jnp.concatenate([top.astype(F32), jnp.zeros((16 - groups, HEAD), F32)], axis=0).astype(BF16)
    ref[groups * GROUP:groups * GROUP + 16, :] = top


def decode(ref, rows):
    groups = rows // GROUP
    y = ref[0:rows, :].astype(F32).reshape(groups, GROUP, HEAD)
    top = ref[rows:rows + 16, :].astype(F32)[0:groups] * (1.0 / MIDDLE)
    k = jnp.floor(jnp.log2(y * (1.0 + 1.0 / 512.0)))
    u = (k + (SHIFT - 1.0 - MIDDLE)) + y * jnp.exp2(-k)
    return (u * top[:, None, :]).reshape(rows, HEAD)


def kernel(
    normed, kw, gain, pk, pv, out_k, out_v,
    x, xt, wk, wv, acc, cot, part, o1, r1, o2, r2, r3, r4, probes, landed,
    load_sem, send_sem, recv_sem,
):
    me = Place()
    a, b, yl, c = me.at["a"], me.at["b"], me.y_lo, me.c
    every = range(4)
    count = [0]
    started = []
    sent = []

    def send(src, dst, device, now=True):
        k = count[0]
        count[0] += 1
        copy = pltpu.make_async_remote_copy(
            src_ref=src, dst_ref=dst, send_sem=send_sem.at[k], recv_sem=recv_sem.at[k],
            device_id=device, device_id_type=MESH,
        )
        started.append(copy)
        if now:
            copy.start()
        return copy

    def same(ref, device):
        return send(ref, ref, device)

    def arrive(*copies):
        for copy in copies:
            copy.wait_recv()

    loads = [
        pltpu.make_async_copy(normed.at[pl.ds(i * 256, 256)], x.at[0, pl.ds(i * 256, 256)], load_sem.at[i])
        for i in range(4)
    ]
    for copy in loads:
        copy.start()

    barrier = pltpu.get_barrier_semaphore()
    greeted = [me.device(axis, d) for axis in ("a", "b", "y") for d in (1, 2, 3)]
    greeted += [me.device(axis, d, True) for axis in ("a", "b", "y") for d in (1, 2, 3)]
    greeted.append(me.sibling())
    for device in greeted:
        pl.semaphore_signal(barrier, inc=1, device_id=device, device_id_type=MESH)

    to = {(axis, d): me.device(axis, d) for axis in ("a", "b", "y") for d in (1, 2, 3)}
    AP, AM, BP, BM, YP, YM = (to[k] for k in (("a", 1), ("a", 3), ("b", 1), ("b", 3), ("y", 1), ("y", 3)))
    am, ap, bm, bp = (a + 3) % 4, (a + 1) % 4, (b + 3) % 4, (b + 1) % 4
    ao, bo, yo = (a + 2) % 4, (b + 2) % 4, 1 - yl
    sibling = me.sibling()

    class Gather:
        def __init__(self, w):
            self.w = w
            self.h0, self.h1 = pl.ds(0, HEAD // 2), pl.ds(HEAD // 2, HEAD // 2)

        def over_y(self, at):
            w = self.w
            return same(w.at[0, :, at, yl, self.h0], YP), same(w.at[0, :, at, yl, self.h1], YM)

        def start(self):
            w = self.w
            self.c0 = [same(w.at[0, a, b, yl], to["a", d]) for d in (2, 1, 3)]
            self.d0 = [same(w.at[1, a, b, yl], to["b", d]) for d in (2, 1, 3)]

        def c1(self):
            arrive(*self.c0)
            self.c = same(self.w.at[0, :, b, yl], BP), same(self.w.at[0, :, b, yl], BM)

        def y0(self):
            self.near = self.over_y(b)

        def e0(self):
            arrive(*self.d0)
            w = self.w
            self.e = same(w.at[1, a, :, yl, self.h0], YP), same(w.at[1, a, :, yl, self.h1], YM)

        def s0(self):
            self.s = same(self.w.at[1, a, :, yl], AP), same(self.w.at[1, a, :, yl], AM)

        def s1(self):
            arrive(*self.e)
            self.r = same(self.w.at[1, a, :, yo], AP), same(self.w.at[1, a, :, yo], AM)

        def f1(self):
            w = self.w
            arrive(*self.c)
            self.f = same(w.at[0, :, bm, yl, self.h0], BP), same(w.at[0, :, bp, yl, self.h1], BM)

        def y1(self):
            self.beside = self.over_y(bm) + self.over_y(bp)

        def t0(self):
            w = self.w
            arrive(*self.s)
            self.t = same(w.at[1, am, :, yl, self.h0], AP), same(w.at[1, ap, :, yl, self.h1], AM)

        def t1(self):
            w = self.w
            arrive(*self.r)
            self.u = same(w.at[1, am, :, yo, self.h0], AP), same(w.at[1, ap, :, yo, self.h1], AM)

        def y2(self):
            arrive(*self.f)
            self.far = self.over_y(bo)

    keys, values = Gather(wk), Gather(wv)

    for h in range(2):
        cols = pl.ds(pl.multiple_of(c * 256 + h * HEAD, HEAD), HEAD)
        wk[h, a, b, yl, :, 0:HEAD] = kw[:, cols]
        wk[h, a, b, yl, :, HEAD:2 * HEAD] = pk[:, cols]
        wv[h, a, b, yl] = pv[:, cols]
    pl.semaphore_wait(barrier, len(greeted))
    pair = [send(normed.at[pl.ds(i * 256, 256)], x.at[1, pl.ds(i * 256, 256)], sibling) for i in range(4)]
    values.start()
    keys.start()
    for copy in loads:
        copy.wait()

    def turn(half, blocks):
        for k in blocks:
            xt[half, 4 * k:4 * k + 4] = x[half, :, k * HEAD:(k + 1) * HEAD].T.reshape(4, 32, ROWS)

    def piece(h, halves, shards, first=False, turned=()):
        def add(half):
            lhs = jnp.concatenate(
                [x[half, :, pl.ds(pl.multiple_of(me.shard(i, j, k) * HEAD, HEAD), HEAD)] for i, j, k in shards], axis=1
            )
            rhs = jnp.concatenate([wk[h, i, j, k] for i, j, k in shards], axis=0)
            new = jnp.dot(lhs, rhs, preferred_element_type=F32)
            for k in range(2):
                some = new[:, k * HEAD:(k + 1) * HEAD].reshape(16, 64, HEAD)
                if first:
                    acc[h, half, k] = some
                else:
                    acc[h, half, k] += some

        if len(halves) == 1:
            turn(halves[0], turned)
            add(halves[0])
        else:
            pl.loop(0, 2)(add)

    def cot_k():
        @pl.loop(0, 8)
        def _(n):
            half, at = n // 4, pl.ds((n % 4) * 4, 4)
            g = gain[...]
            for h in range(2):
                alpha = acc[h, half, 0, at].reshape(256, HEAD)
                delta = acc[h, half, 1, at].reshape(256, HEAD)
                inv = lax.rsqrt(jnp.mean(alpha * alpha, axis=1, keepdims=True) + EPS)
                cubed = inv * inv * inv
                along = jnp.sum(alpha * delta, axis=1, keepdims=True) / HEAD
                gt = g * (g * (delta * inv - alpha * (along * cubed)))
                back = gt * inv - alpha * ((jnp.sum(alpha * gt, axis=1, keepdims=True) / HEAD) * cubed)
                cot[pl.ds(pl.multiple_of(n * 256, 256), 256), (2 + h) * HEAD:(3 + h) * HEAD] = back.astype(BF16)

    def cot_v(half):
        @pl.loop(0, 2)
        def _(n):
            at = pl.ds(pl.multiple_of(n * 512, 512), 512)
            rhs = jnp.concatenate(
                [
                    jnp.concatenate([wv[h, i, j, k] for s in range(16) for i, j in (me.xz(s // 4, s % 4),) for k in range(2)], axis=0)
                    for h in range(2)
                ],
                axis=1,
            )
            new = jnp.dot(x[half, at, :], rhs, preferred_element_type=F32)
            cot[pl.ds(pl.multiple_of(half * ROWS + n * 512, 512), 512), 0:2 * HEAD] = new.astype(BF16)

    axes = (("a", "y", "b"), ("a", "b", "y"), ("a", "y", "b"), ("a", "b", "y"))
    first = [{} for _ in axes]

    plan = ((2, 0, 1), (2, 1, 3), (1, 1, 1), (3, 0, 3), (1, 0, 1), (3, 1, 3))

    def kept(q):
        return part.at[q] if q < 2 else acc.at[q - 2, 0]

    def product(q1, step):
        i1 = (me.at["a"] + step) % 4
        blocks = [me.block(i1, k, j, core) for j in every for k in every for core in range(2)]
        lhs = jnp.concatenate([jnp.concatenate([xt[half, k] for k in blocks], axis=0) for half in range(2)], axis=1)
        new = jnp.dot(lhs, cot[:, q1 * HEAD:(q1 + 2) * HEAD], preferred_element_type=F32)
        one = new[:, 0:HEAD]
        two = new[:, HEAD:2 * HEAD].reshape(4, 4, 64, HEAD)
        two = jnp.concatenate([two[j, k] for k in every for j in every], axis=0)
        for q, rows in ((q1, one), (q1 + 1, two)):
            if step == 0:
                kept(q)[0] = rows.reshape(16, 64, HEAD)
                continue
            for slot, (chunk, half, way) in enumerate(plan):
                if chunk != step:
                    continue
                some = rows[half * 512:(half + 1) * 512]
                if slot < 4:
                    ship(q, slot, some)
                else:
                    kept(q)[1, 8 * slot - 32:8 * slot - 24] = some.reshape(8, 64, HEAD)

    def ship(q, slot, rows):
        encode(rows, o1.at[q, slot % 4])
        first[q][slot] = send(o1.at[q, slot % 4], r1.at[q, slot], to["a", plan[slot][2]])

    def relay(q):
        for slot in (4, 5):
            first[q][slot - 4].wait_recv()
            first[q][slot - 4].wait_send()
            sent.append(first[q][slot - 4])
            own = kept(q)[1, 8 * slot - 32:8 * slot - 24].reshape(512, HEAD)
            ship(q, slot, own + decode(r1.at[q, slot - 4], 512))

    s = [None] * 4
    t = [None] * 4
    final = [None] * 4

    def second(q):
        for half, slots in ((0, (3, 4)), (1, (2, 5))):
            at = slice(8 * half, 8 * half + 8)
            total = kept(q)[0, at].reshape(512, HEAD)
            for slot in slots:
                first[q][slot].wait_recv()
                total = total + decode(r1.at[q, slot], 512)
            kept(q)[0, at] = total.reshape(8, 64, HEAD)
        j = me.at[axes[q][1]]
        s[q] = []
        for d in (2, 1, 3):
            encode(kept(q)[0, pl.ds(((j + d) % 4) * 4, 4)].reshape(256, HEAD), o2.at[q, d - 1])
            s[q].append(send(o2.at[q, d - 1], r2.at[q, d - 1], to[axes[q][1], d]))

    def third(q):
        j, k = me.at[axes[q][1]], me.at[axes[q][2]]
        at = pl.ds(j * 4, 4)
        total = kept(q)[0, at].reshape(256, HEAD)
        for n, d in enumerate((2, 1, 3)):
            s[q][n].wait_recv()
            total = total + decode(r2.at[q, d - 1], 256)
        kept(q)[0, at] = total.reshape(4, 64, HEAD)
        axis = axes[q][2]
        rows, others = pl.ds(pl.multiple_of(c * 32, 32), 32), pl.ds(pl.multiple_of((1 - c) * 32, 32), 32)
        t[q] = [send(kept(q).at[0, j * 4 + (k + d) % 4, rows], r3.at[q, d - 1], to[axis, d]) for d in (2, 1, 3)]
        final[q] = [
            send(kept(q).at[0, j * 4 + (k + d) % 4, others], r4.at[q, d - 1], me.device(axis, d, True)) for d in (2, 1, 3)
        ]
        final[q].append(send(kept(q).at[0, j * 4 + k, others], r4.at[q, 3], sibling))

    def last(q):
        arrive(*t[q])
        rows = pl.ds(pl.multiple_of(c * 32, 32), 32)
        total = kept(q)[0, me.at[axes[q][1]] * 4 + me.at[axes[q][2]], rows] + r3[q, 0] + r3[q, 1] + r3[q, 2]
        put(q, c, total * probes[c, q])

    def put(q, core, total):
        out = out_v if q < 2 else out_k
        out[:, pl.ds(pl.multiple_of(core * 256 + (q % 2) * HEAD, HEAD), HEAD)] = total * (1.0 / TOKENS)

    def rows_of_probes():
        for core in range(2):
            n = (me.y_hi * 2 + core) * 8 + me.fs // 4
            i, j = me.xz(n // 8, (n // 2) % 4)
            row = pl.ds(pl.multiple_of((me.fs % 4) * 32, 32), 32)
            for q in range(4):
                rows = wv[q, i, j, n % 2, row, :] if q < 2 else wk[q - 2, i, j, n % 2, row, HEAD:2 * HEAD]
                probes[core, q] = rows.astype(F32)

    values.c1()
    values.y0()
    values.e0()
    values.s0()
    keys.c1()
    keys.y0()
    values.s1()
    keys.e0()
    piece(0, (0,), [(i, b, yl) for i in every], first=True, turned=range(0, 4))
    values.f1()
    keys.s0()
    piece(1, (0,), [(a, j, yl) for j in every], first=True, turned=range(4, 8))
    arrive(*keys.near)
    piece(0, (0,), [(i, b, yo) for i in every], turned=range(12, 16))
    values.y1()
    arrive(*pair)
    values.y2()
    values.t0()
    keys.f1()
    piece(0, (0,), [(i, j, yl) for i in every for j in (bm, bp)], turned=range(24, 32))
    values.t1()
    piece(0, (1,), [(i, b, k) for i in every for k in (yl, yo)]
          + [(i, j, yl) for i in every for j in (bm, bp)], first=True, turned=range(16, 32))
    keys.y1()
    keys.s1()
    piece(1, (0,), [(a, j, yo) for j in every], turned=range(8, 12))
    keys.t0()
    piece(1, (0,), [(i, j, yl) for i in (am, ap) for j in every], turned=range(16, 24))
    piece(1, (1,), [(a, j, k) for j in every for k in (yl, yo)]
          + [(i, j, yl) for i in (am, ap) for j in every], first=True, turned=range(0, 16))
    arrive(*values.near, *values.beside, *values.far, *values.t, *values.u)
    cot_v(0)
    cot_v(1)
    keys.t1()
    piece(1, (0, 1), [(i, j, yo) for i in (am, ap) for j in every])
    arrive(*keys.beside)
    piece(0, (0, 1), [(i, j, yo) for i in every for j in (bm, bp)])
    keys.y2()
    product(0, 2)
    product(0, 1)
    product(0, 3)
    arrive(*keys.t, *keys.u)
    piece(1, (0, 1), [(ao, j, k) for j in every for k in (yl, yo)])
    arrive(*keys.far)
    piece(0, (0, 1), [(i, bo, k) for i in every for k in (yl, yo)])
    rows_of_probes()
    shared = send(probes.at[1 - c], landed, sibling)
    cot_k()
    relay(0)
    product(2, 2)
    product(2, 1)
    product(2, 3)
    product(0, 0)
    relay(1)
    second(0)
    relay(3)
    product(2, 0)
    relay(2)
    second(1)
    second(3)
    second(2)
    third(3)
    third(1)
    third(0)
    third(2)
    last(0)
    last(3)
    last(1)
    last(2)
    arrive(shared)
    for q in (0, 1, 2, 3):
        arrive(*final[q])
        put(q, 1 - c, (r4[q, 0] + r4[q, 1] + r4[q, 2] + r4[q, 3]) * landed[q])
    for copy in started:
        if not any(copy is other for other in sent):
            copy.wait_send()
    assert count[0] == N_REMOTE


def hand_over(k_ref, v_ref, out_k, out_v):
    out_k[...] = k_ref[...]
    out_v[...] = v_ref[...]


def shards(normed, k_weight, k_gain, probe_k, probe_v):
    vmem = pl.BlockSpec(memory_space=pltpu.VMEM)
    out = jax.ShapeDtypeStruct((32, 512), F32)
    diag_k, diag_v = pl.pallas_call(
        kernel,
        name="curvature",
        out_shape=(out, out),
        in_specs=[pl.BlockSpec(memory_space=pl.ANY)] + [vmem] * 4,
        out_specs=(vmem, vmem),
        scratch_shapes=[
            pltpu.VMEM((2, ROWS, 32 * HEAD), BF16),
            pltpu.VMEM((2, 128, 32, ROWS), BF16),
            pltpu.VMEM((2, 4, 4, 2, HEAD, 2 * HEAD), BF16),
            pltpu.VMEM((2, 4, 4, 2, HEAD, HEAD), BF16),
            pltpu.VMEM((2, 2, 2, 16, 64, HEAD), F32),
            pltpu.VMEM((2 * ROWS, 4 * HEAD), BF16),
            pltpu.VMEM((2, 2, 16, 64, HEAD), F32),
            pltpu.VMEM((4, 4, 528, HEAD), BF16),
            pltpu.VMEM((4, 6, 528, HEAD), BF16),
            pltpu.VMEM((4, 3, 272, HEAD), BF16),
            pltpu.VMEM((4, 3, 272, HEAD), BF16),
            pltpu.VMEM((4, 3, 32, HEAD), F32),
            pltpu.VMEM((4, 4, 32, HEAD), F32),
            pltpu.VMEM((2, 4, 32, HEAD), F32),
            pltpu.VMEM((4, 32, HEAD), F32),
            pltpu.SemaphoreType.DMA((4,)),
            pltpu.SemaphoreType.DMA((N_REMOTE,)),
            pltpu.SemaphoreType.DMA((N_REMOTE,)),
        ],
        compiler_params=pltpu.CompilerParams(
            collective_id=0, has_side_effects=True, vmem_limit_bytes=63 * 2**20
        ),
        cost_estimate=pl.CostEstimate(flops=21 * 10**9, bytes_accessed=10**7, transcendentals=0),
    )(normed, k_weight, k_gain.reshape(1, HEAD), probe_k, probe_v)
    return pl.pallas_call(
        hand_over,
        name="hand_over",
        out_shape=(out, out),
        in_specs=[vmem, vmem],
        out_specs=(vmem, vmem),
    )(diag_k, diag_v)


def solution(mesh):
    return jax.shard_map(
        shards,
        mesh=mesh,
        in_specs=(P(("dp", "fsdp"), None), P("fsdp", None), P(), P("fsdp", None), P("fsdp", None)),
        out_specs=(P(("dp", "fsdp"), None), P(("dp", "fsdp"), None)),
        check_vma=False,
    )
```
